256 devices in a mesh: row: 8 (over x, core), col: 8 (over z_lo, y), rep: 4 (over z_hi).
Axes of the slice: x: 4, y: 4, z: 8 (z_hi: 4, z_lo: 2; z = z_hi * 2 + z_lo), core: 2. Of those that a mesh axis runs over, the one named last changes fastest.
Arguments:
- left_panel: float32 [1024, 16384], P(('col', 'rep'), 'row'), may hold values from -0.1875 to 0.1875
- right_panel: float32 [8, 4, 32, 16384], P(None, 'rep', 'row', 'col'), may hold values from -6 to 6
- left_mask: int32 [8, 128], replicated, may hold values from 0 to 1, as said below
- right_mask: int32 [8, 128], replicated, may hold values from 0 to 1, as said below
- accum: float32 [16384, 16384], P('row', ('col', 'rep')), may hold values from -6 to 6
Outputs:
- cube_acc: float32 [16384, 16384], P('row', ('col', 'rep'))
The draws below stay inside these ranges and needn't reach their ends.
Inputs may be any that keep to these rules, and one draw needn't show every extreme that they name: `left_mask`: 1 marks an occupied tile, 0 an empty one. `right_mask`: 1 marks an occupied tile, 0 an empty one.
All inputs are finite; a program needn't handle non-finite values.
Results may differ from the reference program's by a relative error of at most 0.00005.
Values sent between devices are 32-bit elements; how exact they have to be, the bound alone decides.
No kernel may reach another device: no remote copies, remote signals or barrier semaphores. Data moves between devices by JAX's collectives and lax.ppermute only.
A program may use at most 64 MiB of HBM per device.

```python
import jax
import jax.numpy as jnp
from jax import lax

TILE = 128
NWIN = 16384
KW = 1024
GROUPS = 8
LAYERS = 4
STRETCH = 32
OFFSET = 7680


def occupancy(key, near, far):
    ktiles = KW // TILE
    ntiles = NWIN // TILE
    first = OFFSET // TILE
    rows = jnp.arange(ktiles, dtype=jnp.int32)[:, None] + first
    cols = jnp.arange(ntiles, dtype=jnp.int32)[None, :]
    distance = jnp.abs(cols - rows)
    limit = near - (near - far) * distance // max(ntiles, 1)
    draws = jax.random.randint(key, (ktiles, ntiles), 0, 1000)
    return (draws < limit).astype(jnp.int32)


def draw_left_mask(key, part):
    key = jax.random.fold_in(key, 11)
    return occupancy(key, 950, 150)


def draw_right_mask(key, part):
    key = jax.random.fold_in(key, 23)
    return occupancy(key, 990, 300)


def block_scale(rng, dims, shards, least, high):
    def one(dim, shards_of):
        steps = jax.random.uniform(jax.random.fold_in(jax.random.fold_in(rng, 6), dim), (shards_of,), jnp.float32, least / len(shards), high / len(shards))
        return jnp.repeat(jnp.exp(steps), dims[dim] // shards_of).reshape((-1,) + (1,) * (len(dims) - dim - 1))

    level = one(*shards[0])
    for cut in shards[1:]:
        level = level * one(*cut)
    return level


def noise(own_key, dims, deviation, reach, cuts=(), held_as=jnp.bfloat16):
    drawn = deviation * jax.random.normal(own_key, dims, jnp.float32)
    if cuts:
        drawn = drawn * block_scale(own_key, dims, cuts, -0.22, 0.18)
    return jnp.clip(drawn, -reach, reach).astype(held_as)


def setup_inputs(seed: int = 0) -> dict:
    key_of = jax.random.split(jax.random.key(seed), 6)
    return {
        "left_panel": noise(key_of[0], (KW, NWIN), KW ** -0.5, 0.1875, ((0, 32), (1, 8)), jnp.float32),
        "right_panel": noise(key_of[1], (GROUPS, LAYERS, STRETCH, NWIN), 1.0, 6.0, ((1, 4), (2, 8), (3, 8)), jnp.float32),
        "left_mask": draw_left_mask(jax.random.fold_in(key_of[5], 71), 0),
        "right_mask": draw_right_mask(jax.random.fold_in(key_of[5], 71), 0),
        "accum": noise(key_of[4], (NWIN, NWIN), 1.0, 6.0, ((0, 8), (1, 32)), jnp.float32),
    }


def expand(mask):
    tiles = jnp.repeat(mask.astype(jnp.float32), TILE, axis=0)
    return jnp.repeat(tiles, TILE, axis=1)


def reference(left_panel, right_panel, left_mask, right_mask, accum):
    masked_left = left_panel * expand(left_mask)
    masked_right = right_panel.reshape(KW, NWIN) * expand(right_mask)
    product = lax.dot_general(masked_left, masked_right, (((0,), (0,)), ((), ())), precision=lax.Precision.HIGHEST, preferred_element_type=jnp.float32)
    return accum + product
```

```python
import functools

import jax
import jax.numpy as jnp
from jax import lax
from jax.experimental import pallas as pl
from jax.experimental.pallas import tpu as pltpu
from jax.sharding import Mesh, PartitionSpec as P

KT = 128
Z = ("zlo", "zhi")
CA = 768
TN = 256


def z_slot(z):
    return (z % 2) * 4 + z // 2


def ring(n, step, slot=lambda i: i):
    return [(slot(i), slot((i + step) % n)) for i in range(n)]


def along_y(a, step):
    return lax.ppermute(a, "y", ring(4, step))


def along_z(a, step):
    return lax.ppermute(a, Z, ring(8, step, z_slot))


def along_x(a, step):
    return lax.ppermute(a, "x", ring(4, step))


def gather_y(own):
    half = own.shape[0] // 2
    up, down = along_y(own, 1), along_y(own, -1)
    return [own, up, down, along_y(up[:half], 1), along_y(down[half:], -1)]


def gather_z(own):
    half = own.shape[0] // 2
    up, down = [own], [own]
    for _ in range(3):
        up.append(along_z(up[-1], 1))
        down.append(along_z(down[-1], -1))
    last = [along_z(up[-1][:half], 1), along_z(down[-1][half:], -1)]
    return [own] + up[1:] + down[1:] + last


def right_kernel(place, own, up, down, far_a, far_b, mask, hi, lo, rows):
    x, rep = place[0], place[1]
    whole, front, back = range(4), range(2), range(2, 4)
    for dx, ref, sent in ((0, own, whole), (-1, up, whole), (1, down, whole), (2, far_a, front), (2, far_b, back)):
        for slot, s in enumerate(sent):
            base = lax.rem(rep - s + 4, 4) * 32 + lax.rem(x + dx + 4, 4) * 8
            for g in range(8):
                rows[pl.ds(pl.multiple_of(g * 128 + base, 8), 8), :] = ref[slot, g]
    for g in range(8):
        at = pl.ds(g * 128, 128)
        a = rows[at, :] * mask[pl.ds(g, 1), :]
        h = a.astype(jnp.bfloat16)
        hi[at, :] = h
        lo[at, :] = (a - h.astype(jnp.float32)).astype(jnp.bfloat16)


def assemble_right(place, pieces, mask):
    vm = pl.BlockSpec(memory_space=pltpu.VMEM)
    return pl.pallas_call(
        right_kernel,
        out_shape=[jax.ShapeDtypeStruct((1024, 512), jnp.bfloat16)] * 2,
        in_specs=[pl.BlockSpec(memory_space=pltpu.SMEM)] + [vm] * 6,
        out_specs=[vm, vm],
        scratch_shapes=[pltpu.VMEM((1024, 512), jnp.float32)],
        compiler_params=pltpu.CompilerParams(vmem_limit_bytes=24 * 2**20),
    )(place, *pieces, mask)


def product_kernel(heights, blocks, *refs):
    n = len(heights)
    pieces = refs[:n]
    mask, hi, lo, accum = refs[n : n + 4]
    out, lhi, llo = refs[-3:]
    j = 0
    for ref, height in zip(pieces, heights):
        for r in range(0, height, 32):
            kb = blocks[j]
            j += 1
            a = ref[r : r + 32, :] * mask[pl.ds(kb // 4, 1), :]
            h = a.astype(jnp.bfloat16)
            at = pl.ds(pl.multiple_of(kb * 32, 32), 32)
            lhi[at, :] = h
            llo[at, :] = (a - h.astype(jnp.float32)).astype(jnp.bfloat16)
    dot = functools.partial(
        lax.dot_general, dimension_numbers=(((0,), (0,)), ((), ())), preferred_element_type=jnp.float32
    )
    total = dot(lhi[...], lo[...]) + dot(llo[...], hi[...])
    out[...] = accum[...] + (total + dot(lhi[...], hi[...]))


def product(blocks, pieces, mask, hi, lo, accum, first, prev=None):
    heights = tuple(p.shape[0] for p in pieces)
    width = pieces[0].shape[1]
    skip = first // TN
    n = len(pieces)

    def wrapped(blocks_ref, *refs):
        refs = list(refs)
        if prev is not None:
            del refs[n + 4]
        product_kernel(heights, blocks_ref, *refs)

    in_specs = [pl.BlockSpec((h, TN), lambda i, b: (0, i)) for h in heights]
    in_specs += [
        pl.BlockSpec((8, TN), lambda i, b: (0, i + skip)),
        pl.BlockSpec((1024, 512), lambda i, b: (0, 0)),
        pl.BlockSpec((1024, 512), lambda i, b: (0, 0)),
        pl.BlockSpec((TN, 512), lambda i, b: (i + skip, 0)),
    ]
    args = [blocks, *pieces, mask, hi, lo, accum]
    aliases = {}
    if prev is not None:
        in_specs.append(pl.BlockSpec(memory_space=pl.ANY))
        aliases = {len(args): 0}
        args.append(prev)
    return pl.pallas_call(
        wrapped,
        out_shape=jax.ShapeDtypeStruct(accum.shape, jnp.float32),
        grid_spec=pltpu.PrefetchScalarGridSpec(
            num_scalar_prefetch=1,
            grid=(width // TN,),
            in_specs=in_specs,
            out_specs=pl.BlockSpec((TN, 512), lambda i, b: (i + skip, 0)),
            scratch_shapes=[pltpu.VMEM((1024, TN), jnp.bfloat16)] * 2,
        ),
        input_output_aliases=aliases,
        compiler_params=pltpu.CompilerParams(vmem_limit_bytes=24 * 2**20),
        cost_estimate=pl.CostEstimate(
            flops=2 * 3 * 1024 * width * 512,
            bytes_accessed=1024 * width * 4 + width * 512 * 8 + 2**21,
            transcendentals=0,
        ),
    )(*args)


def body(left, right, left_mask, right_mask, accum):
    x, core, y = (lax.axis_index(a) for a in ("x", "core", "y"))
    zlo, rep = lax.axis_index("zlo"), lax.axis_index("zhi")
    z = rep * 2 + zlo
    row, col = x * 2 + core, zlo * 4 + y

    a_own = jnp.concatenate(gather_y(left[:, :CA]), 0)
    a = gather_z(a_own)
    b_own = jnp.concatenate(gather_z(left[:, CA:]), 0)
    b = gather_y(b_own)

    def block(dy, dz):
        yy, zz = (y + dy) % 4, (z + dz) % 8
        return ((zz % 2) * 4 + yy) * 4 + zz // 2

    z_order = (0, -1, -2, -3, 1, 2, 3, 4)
    y_order = (0, -1, 1, 2)
    a_blocks = jnp.stack([block(dy, dz) for dz in z_order for dy in y_order]).astype(jnp.int32)
    b_blocks = jnp.stack([block(dy, dz) for dy in y_order for dz in z_order]).astype(jnp.int32)

    layers = []
    for s in range(4):
        owner = (rep + s) % 4
        part = lax.dynamic_slice_in_dim(right, owner * 512, 512, 3)[:, 0]
        layers.append(part if s == 0 else lax.ppermute(part, "zhi", ring(4, s)))
    layers = jnp.stack(layers)
    other = lax.ppermute(layers, "core", [(0, 1), (1, 0)])
    first, second = jnp.where(core == 0, layers, other), jnp.where(core == 0, other, layers)
    both = jnp.concatenate([first, second], 2)
    up, down = along_x(both, 1), along_x(both, -1)
    far_a, far_b = along_x(up[:2], 1), along_x(down[2:], -1)
    right_tiles = lax.dynamic_slice(right_mask, (0, col * 16 + rep * 4), (8, 4)).astype(jnp.float32)
    place = jnp.stack([x, rep]).astype(jnp.int32)
    hi, lo = assemble_right(place, [both, up, down, far_a, far_b], jnp.repeat(right_tiles, KT, axis=1))

    left_tiles = lax.dynamic_slice(left_mask, (0, row * 16), (8, 16)).astype(jnp.float32)
    mask = jnp.repeat(left_tiles, KT, axis=1)
    out = product(a_blocks, a, mask, hi, lo, accum, 0)
    return product(b_blocks, b, mask, hi, lo, accum, CA, out)


def solution(mesh):
    fine = Mesh(mesh.devices.reshape(4, 2, 2, 4, 4), ("x", "core", "zlo", "y", "zhi"))
    row, col, rep = ("x", "core"), ("zlo", "y"), ("zhi",)
    return jax.shard_map(
        body,
        mesh=fine,
        in_specs=(P(col + rep, row), P(None, rep, row, col), P(), P(), P(row, col + rep)),
        out_specs=P(row, col + rep),
        check_vma=False,
    )
```

```python
import functools

import jax
import jax.numpy as jnp
from jax import lax
from jax.experimental import pallas as pl
from jax.experimental.pallas import tpu as pltpu
from jax.sharding import Mesh, PartitionSpec as P

KT = 128
RUN = 16
Z = ("zlo", "zhi")
VMEM = 56 * 2**20
TN = 512


def z_slot(z):
    return (z % 2) * 4 + z // 2


def ring(n, step, slot=lambda i: i):
    return [(slot(i), slot((i + step) % n)) for i in range(n)]


def along_x(a):
    pairs = [(i * 2 + c, (i + 1 - 2 * c) % 4 * 2 + c) for i in range(4) for c in (0, 1)]
    return lax.ppermute(a, ("x", "core"), pairs)


def other_core(a):
    return lax.ppermute(a, "core", [(0, 1), (1, 0)])


def place_of(core, z, y):
    return ((core * 2 + z % 2) * 4 + y) * 4 + z // 2


def cross(a, step, cores=(0, 1), flip=False):
    pairs = []
    for z in range(8):
        for y in range(4):
            for c in cores:
                to = (c, z, (y + step) % 4) if (c == 0) != flip else (c, (z + step) % 8, y)
                pairs.append((place_of(c, z, y), place_of(*to)))
    return lax.ppermute(a, ("core", "zlo", "y", "zhi"), pairs)


def after(a, *others):
    return lax.optimization_barrier((a,) + others)[0]


def split(a):
    h = a.astype(jnp.bfloat16)
    return h, (a - h.astype(jnp.float32)).astype(jnp.bfloat16)


def right_kernel(place, own, near, near_o, far, far_o, mask, hi, lo, rows, *refs):
    parts, sems = refs[:5], refs[5]
    x, core, rep = place[0], place[1], place[2]
    step = 2 * core - 1
    origins = ((x, 0), (x + step, 0), (x - step, 0), (x + 2, 2 * core), (x + 2, 2 - 2 * core))
    sources = (own, near, near_o, far, far_o)
    copies = [pltpu.make_async_copy(a, b, sems.at[i]) for i, (a, b) in enumerate(zip(sources, parts))]
    for copy in copies:
        copy.start()
    for copy, ref, (at_x, first) in zip(copies, parts, origins):
        copy.wait()
        for slot in range(ref.shape[0]):
            base = lax.rem(rep - first - slot + 4, 4) * 32 + lax.rem(at_x + 4, 4) * 8
            for g in range(8):
                rows[pl.ds(pl.multiple_of(g * 128 + base, 8), 8), :] = ref[slot, g]
    for g in range(8):
        at = pl.ds(g * 128, 128)
        hi[at, :], lo[at, :] = split(rows[at, :] * mask[pl.ds(g, 1), :])


def assemble_right(place, sources, mask):
    vm, hbm = pl.BlockSpec(memory_space=pltpu.VMEM), pl.BlockSpec(memory_space=pl.ANY)
    return pl.pallas_call(
        right_kernel,
        out_shape=[jax.ShapeDtypeStruct((1024, 512), jnp.bfloat16)] * 2,
        in_specs=[pl.BlockSpec(memory_space=pltpu.SMEM)] + [hbm] * 5 + [vm],
        out_specs=[vm, vm],
        scratch_shapes=[pltpu.VMEM((1024, 512), jnp.float32)]
        + [pltpu.VMEM(a.shape, jnp.float32) for a in sources]
        + [pltpu.SemaphoreType.DMA((5,))],
        compiler_params=pltpu.CompilerParams(vmem_limit_bytes=VMEM),
    )(place, *sources, mask)


def product_kernel(heights, runs, *refs):
    n = len(heights)
    tiles = 2048 // TN
    pieces, refs = refs[:n], refs[n:]
    mask, hi_in, lo_in, accum, out = refs[:5]
    held, refs = refs[5 : 5 + n], refs[5 + n :]
    hi, lo, lhi, llo, total, piece_sems, in_sems, out_sems, right_sems = refs

    def tile(i):
        return pl.ds(i * TN, TN)

    def fetches(i):
        cols = tile(i)
        copies = [
            pltpu.make_async_copy(a.at[:, cols], b.at[:, cols], piece_sems.at[i, k])
            for k, (a, b) in enumerate(zip(pieces, held))
        ]
        return copies, pltpu.make_async_copy(accum.at[cols], total.at[i], in_sems.at[i])

    right_in = [pltpu.make_async_copy(a, b, right_sems.at[i]) for i, (a, b) in enumerate(((hi_in, hi), (lo_in, lo)))]
    sends = [pltpu.make_async_copy(total.at[i], out.at[tile(i)], out_sems.at[i]) for i in range(tiles)]
    loads = [fetches(i) for i in range(tiles)]
    for copy in loads[0][0] + right_in + [loads[0][1]]:
        copy.start()
    dot = functools.partial(
        lax.dot_general, dimension_numbers=(((0,), (0,)), ((), ())), preferred_element_type=jnp.float32
    )

    def prepare(i):
        cols, slot = tile(i), i % 2
        j = 0
        for ref, height in zip(held, heights):
            for r in range(0, height, RUN):
                run = runs[j]
                there = pl.ds(pl.multiple_of(run * RUN, RUN), RUN)
                a = ref[r : r + RUN, cols] * mask[pl.ds(run // (KT // RUN), 1), cols]
                lhi[slot, there, :], llo[slot, there, :] = split(a)
                j += 1

    for copy in loads[1][0] + [loads[1][1]]:
        copy.start()
    for copy in loads[0][0]:
        copy.wait()
    prepare(0)
    for copy in right_in:
        copy.wait()
    for i in range(tiles):
        if i + 2 < tiles:
            for copy in loads[i + 2][0] + [loads[i + 2][1]]:
                copy.start()
        if i + 1 < tiles:
            for copy in loads[i + 1][0]:
                copy.wait()
        loads[i][1].wait()
        left_hi, left_lo = lhi[i % 2, :1024, :], llo[i % 2, :1024, :]
        add = dot(left_hi, lo[...]) + dot(left_lo, hi[...])
        if i + 1 < tiles:
            prepare(i + 1)
        add = add + dot(left_hi, hi[...])
        total[i] = total[i] + add
        sends[i].start()
    for copy in sends:
        copy.wait()


def product(runs, pieces, mask, hi, lo, accum):
    heights = tuple(p.shape[0] for p in pieces)
    width = pieces[0].shape[1]
    depth = sum(heights)
    tiles = width // TN
    vm, hbm = pl.BlockSpec(memory_space=pltpu.VMEM), pl.BlockSpec(memory_space=pl.ANY)
    sems = pltpu.SemaphoreType.DMA
    scratch = [pltpu.VMEM(p.shape, jnp.float32) for p in pieces]
    scratch += [pltpu.VMEM((1024, 512), jnp.bfloat16)] * 2 + [pltpu.VMEM((2, depth, TN), jnp.bfloat16)] * 2
    scratch += [pltpu.VMEM((tiles, TN, 512), jnp.float32), sems((tiles, len(pieces)))]
    scratch += [sems((tiles,)), sems((tiles,)), sems((2,))]
    return pl.pallas_call(
        functools.partial(product_kernel, heights),
        out_shape=jax.ShapeDtypeStruct(accum.shape, jnp.float32),
        in_specs=[pl.BlockSpec(memory_space=pltpu.SMEM)] + [hbm] * len(pieces) + [vm, hbm, hbm, hbm],
        out_specs=hbm,
        scratch_shapes=scratch,
        compiler_params=pltpu.CompilerParams(vmem_limit_bytes=VMEM),
        cost_estimate=pl.CostEstimate(
            flops=2 * 3 * 1024 * width * 512,
            bytes_accessed=depth * width * 4 + width * 512 * 8 + 2**21,
            transcendentals=0,
        ),
    )(runs, *pieces, mask, hi, lo, accum)


def body(left, right, left_mask, right_mask, accum):
    x, core, y = (lax.axis_index(a) for a in ("x", "core", "y"))
    zlo, rep = lax.axis_index("zlo"), lax.axis_index("zhi")
    z = rep * 2 + zlo
    row, col = x * 2 + core, zlo * 4 + y

    zero = core == 0

    def pick(a, b):
        return jnp.where(zero, a, b)

    def join(*parts):
        return jnp.concatenate(parts, 0)

    s1u, s1d = cross(left, 1), cross(left, -1)
    s2u, s2d = cross(s1u, 1), cross(s1d, -1, (1,))

    m1 = join(left, s1u, s1d, s2u)
    u1, d1 = cross(m1, 1, flip=True), cross(m1, -1, flip=True)
    s3u, s3d = cross(s2u, 1, (1,)), cross(s2d, -1, (1,))
    s4 = cross(s3u, 1, (1,))

    layers = []
    for s in range(4):
        owner = (rep + s) % 4
        part = lax.dynamic_slice_in_dim(right, owner * 512, 512, 3)[:, 0]
        layers.append(part if s == 0 else lax.ppermute(part, "zhi", ring(4, s)))

    layers = jnp.stack(layers)
    other = other_core(layers)
    both = jnp.concatenate([pick(layers, other), pick(other, layers)], 2)
    near = along_x(both)
    near_o = other_core(near)
    far = along_x(pick(near[:2], near[2:]))
    far_o = other_core(far)

    m2 = join(s2d, s3u, s3d, s4)
    u2, d2 = cross(pick(u1, m2), 1, flip=True), cross(pick(d1, m2), -1, flip=True)
    u3a, d3b = cross(pick(u2[:64], u1[:64]), 1, flip=True), cross(d2[64:], -1, flip=True)
    u3b, d3a = cross(pick(u2[64:], u2[:64]), 1, flip=True), cross(pick(d2[:64], d1[64:]), -1, flip=True)

    def run(dy, dz, half):
        yy, zz = (y + dy) % 4, (z + dz) % 8
        return (((zz % 2) * 4 + yy) * 4 + zz // 2) * 2 + half

    def table(core0, core1):
        at, spare = [], [64, 64]
        for pair in zip(core0, core1, strict=True):
            both_at = []
            for c, offsets in enumerate(pair):
                both_at.append(spare[c] if offsets is None else run(*offsets))
                spare[c] += offsets is None
            at.append(pick(*both_at))
        return jnp.stack(at).astype(jnp.int32)

    def halves(*offsets):
        return [(dy, dz, half) for dy, dz in offsets for half in (0, 1)]

    none = [None, None]
    ones, twos, dys = (0, -1, 1, -2), (2, -3, 3, 4), (0, -1, 1, 2)

    def around_z(dz):
        return halves(*((dy, dz) for dy in dys))

    def around_y(dy, dzs):
        return halves(*((dy, dz) for dz in dzs))

    runs = table(
        halves((0, 0), (-1, 0), (1, 0), (2, 0))
        + none * 4
        + around_z(-1)
        + around_z(1)
        + around_z(-2)
        + around_z(2)
        + around_z(-3)
        + around_z(3)
        + around_z(4),
        halves(*((0, dz) for dz in ones + twos))
        + around_y(-1, ones)
        + around_y(1, ones)
        + around_y(-1, twos)
        + around_y(1, twos)
        + around_y(2, ones)[:4]
        + around_y(2, twos)[:4]
        + around_y(2, ones)[4:]
        + around_y(2, twos)[4:]
        + none * 4,
    )

    right_tiles = lax.dynamic_slice(right_mask, (0, col * 16 + rep * 4), (8, 4)).astype(jnp.float32)
    place = jnp.stack([x, core, rep]).astype(jnp.int32)
    right_mask = jnp.repeat(right_tiles, KT, axis=1)
    left_tiles = lax.dynamic_slice(left_mask, (0, row * 16), (8, 16)).astype(jnp.float32)
    mask = jnp.pad(jnp.repeat(left_tiles, KT, axis=1), ((0, 8), (0, 0)))

    u4, d4 = cross(u3a, 1, (0,), True), cross(d3b, -1, (0,), True)
    hi, lo = assemble_right(after(place, u1, d1), [both, near, near_o, far, far_o], right_mask)
    pieces = [left, s1u, s1d, s2u, s2d, s3u, s3d, s4, u1, d1, u2, d2, u3a, u3b, d3a, d3b, u4, d4]
    return product(runs, pieces, mask, hi, lo, accum)


def solution(mesh):
    fine = Mesh(mesh.devices.reshape(4, 2, 2, 4, 4), ("x", "core", "zlo", "y", "zhi"))
    row, col, rep = ("x", "core"), ("zlo", "y"), ("zhi",)
    return jax.shard_map(
        body,
        mesh=fine,
        in_specs=(P(col + rep, row), P(None, rep, row, col), P(), P(), P(row, col + rep)),
        out_specs=P(row, col + rep),
        check_vma=False,
    )
```

```python
import functools

import jax
import jax.numpy as jnp
from jax import lax
from jax.experimental import pallas as pl
from jax.experimental.pallas import tpu as pltpu
from jax.sharding import Mesh, PartitionSpec as P

KT = 128
RUN = 16
Z = ("zlo", "zhi")
VMEM = 56 * 2**20
TN = 512


def z_slot(z):
    return (z % 2) * 4 + z // 2


def ring(n, step, slot=lambda i: i):
    return [(slot(i), slot((i + step) % n)) for i in range(n)]


def along_x(a):
    pairs = [(i * 2 + c, (i + 1 - 2 * c) % 4 * 2 + c) for i in range(4) for c in (0, 1)]
    return lax.ppermute(a, ("x", "core"), pairs)


def other_core(a):
    return lax.ppermute(a, "core", [(0, 1), (1, 0)])


def place_of(core, z, y):
    return ((core * 2 + z % 2) * 4 + y) * 4 + z // 2


def cross(a, step, cores=(0, 1), flip=False):
    pairs = []
    for z in range(8):
        for y in range(4):
            for c in cores:
                to = (c, z, (y + step) % 4) if (c == 0) != flip else (c, (z + step) % 8, y)
                pairs.append((place_of(c, z, y), place_of(*to)))
    return lax.ppermute(a, ("core", "zlo", "y", "zhi"), pairs)


def after(a, *others):
    return lax.optimization_barrier((a,) + others)[0]


def split(a):
    h = a.astype(jnp.bfloat16)
    return h, (a - h.astype(jnp.float32)).astype(jnp.bfloat16)


def right_kernel(place, own, near, near_o, far, far_o, mask, hi, lo, rows, *refs):
    parts, sems = refs[:5], refs[5]
    x, core, rep = place[0], place[1], place[2]
    step = 2 * core - 1
    origins = ((x, 0), (x + step, 0), (x - step, 0), (x + 2, 2 * core), (x + 2, 2 - 2 * core))
    sources = (own, near, near_o, far, far_o)
    copies = [pltpu.make_async_copy(a, b, sems.at[i]) for i, (a, b) in enumerate(zip(sources, parts))]
    for copy in copies:
        copy.start()
    for copy, ref, (at_x, first) in zip(copies, parts, origins):
        copy.wait()
        for slot in range(ref.shape[0]):
            base = lax.rem(rep - first - slot + 4, 4) * 32 + lax.rem(at_x + 4, 4) * 8
            for g in range(8):
                rows[pl.ds(pl.multiple_of(g * 128 + base, 8), 8), :] = ref[slot, g]
    for g in range(8):
        at = pl.ds(g * 128, 128)
        hi[at, :], lo[at, :] = split(rows[at, :] * mask[pl.ds(g, 1), :])


def assemble_right(place, sources, mask):
    vm, hbm = pl.BlockSpec(memory_space=pltpu.VMEM), pl.BlockSpec(memory_space=pl.ANY)
    return pl.pallas_call(
        right_kernel,
        out_shape=[jax.ShapeDtypeStruct((1024, 512), jnp.bfloat16)] * 2,
        in_specs=[pl.BlockSpec(memory_space=pltpu.SMEM)] + [hbm] * 5 + [vm],
        out_specs=[vm, vm],
        scratch_shapes=[pltpu.VMEM((1024, 512), jnp.float32)]
        + [pltpu.VMEM(a.shape, jnp.float32) for a in sources]
        + [pltpu.SemaphoreType.DMA((5,))],
        compiler_params=pltpu.CompilerParams(vmem_limit_bytes=VMEM),
    )(place, *sources, mask)


def product_kernel(heights, runs, *refs):
    n = len(heights)
    tiles = 2048 // TN
    pieces, refs = refs[:n], refs[n:]
    mask, hi_in, lo_in, accum, out = refs[:5]
    held, refs = refs[5 : 5 + n], refs[5 + n :]
    hi, lo, lhi, llo, total, piece_sems, in_sems, out_sems, right_sems = refs

    def tile(i):
        return pl.ds(i * TN, TN)

    def fetches(i):
        cols = tile(i)
        copies = [
            pltpu.make_async_copy(a.at[:, cols], b.at[:, cols], piece_sems.at[i, k])
            for k, (a, b) in enumerate(zip(pieces, held))
        ]
        return copies, pltpu.make_async_copy(accum.at[cols], total.at[i], in_sems.at[i])

    right_in = [pltpu.make_async_copy(a, b, right_sems.at[i]) for i, (a, b) in enumerate(((hi_in, hi), (lo_in, lo)))]
    sends = [pltpu.make_async_copy(total.at[i], out.at[tile(i)], out_sems.at[i]) for i in range(tiles)]
    loads = [fetches(i) for i in range(tiles)]
    for copy in loads[0][0] + right_in + [loads[0][1]]:
        copy.start()
    dot = functools.partial(
        lax.dot_general, dimension_numbers=(((0,), (0,)), ((), ())), preferred_element_type=jnp.float32
    )

    def prepare(i):
        cols, slot = tile(i), i % 2
        j = 0
        for ref, height in zip(held, heights):
            for r in range(0, height, RUN):
                run = runs[j]
                there = pl.ds(pl.multiple_of(run * RUN, RUN), RUN)
                a = ref[r : r + RUN, cols] * mask[pl.ds(run // (KT // RUN), 1), cols]
                lhi[slot, there, :], llo[slot, there, :] = split(a)
                j += 1

    for copy in loads[1][0] + [loads[1][1]]:
        copy.start()
    for copy in loads[0][0]:
        copy.wait()
    prepare(0)
    for copy in right_in:
        copy.wait()
    for i in range(tiles):
        if i + 2 < tiles:
            for copy in loads[i + 2][0] + [loads[i + 2][1]]:
                copy.start()
        left_hi, left_lo = lhi[i % 2, :1024, :], llo[i % 2, :1024, :]
        add = dot(left_hi, lo[...]) + dot(left_lo, hi[...])
        if i + 1 < tiles:
            for copy in loads[i + 1][0]:
                copy.wait()
            prepare(i + 1)
        add = add + dot(left_hi, hi[...])
        loads[i][1].wait()
        total[i] = total[i] + add
        sends[i].start()
    for copy in sends:
        copy.wait()


def product(runs, pieces, mask, hi, lo, accum):
    heights = tuple(p.shape[0] for p in pieces)
    width = pieces[0].shape[1]
    depth = sum(heights)
    tiles = width // TN
    vm, hbm = pl.BlockSpec(memory_space=pltpu.VMEM), pl.BlockSpec(memory_space=pl.ANY)
    sems = pltpu.SemaphoreType.DMA
    scratch = [pltpu.VMEM(p.shape, jnp.float32) for p in pieces]
    scratch += [pltpu.VMEM((1024, 512), jnp.bfloat16)] * 2 + [pltpu.VMEM((2, depth, TN), jnp.bfloat16)] * 2
    scratch += [pltpu.VMEM((tiles, TN, 512), jnp.float32), sems((tiles, len(pieces)))]
    scratch += [sems((tiles,)), sems((tiles,)), sems((2,))]
    return pl.pallas_call(
        functools.partial(product_kernel, heights),
        out_shape=jax.ShapeDtypeStruct(accum.shape, jnp.float32),
        in_specs=[pl.BlockSpec(memory_space=pltpu.SMEM)] + [hbm] * len(pieces) + [vm, hbm, hbm, hbm],
        out_specs=hbm,
        scratch_shapes=scratch,
        compiler_params=pltpu.CompilerParams(vmem_limit_bytes=VMEM),
        cost_estimate=pl.CostEstimate(
            flops=2 * 3 * 1024 * width * 512,
            bytes_accessed=depth * width * 4 + width * 512 * 8 + 2**21,
            transcendentals=0,
        ),
    )(runs, *pieces, mask, hi, lo, accum)


def body(left, right, left_mask, right_mask, accum):
    x, core, y = (lax.axis_index(a) for a in ("x", "core", "y"))
    zlo, rep = lax.axis_index("zlo"), lax.axis_index("zhi")
    z = rep * 2 + zlo
    row, col = x * 2 + core, zlo * 4 + y

    zero = core == 0

    def pick(a, b):
        return jnp.where(zero, a, b)

    def join(*parts):
        return jnp.concatenate(parts, 0)

    s1u, s1d = cross(left, 1), cross(left, -1)
    s2u, s2d = cross(s1u, 1), cross(s1d, -1, (1,))

    m1 = join(left, s1u, s1d, s2u)
    u1, d1 = cross(m1, 1, flip=True), cross(m1, -1, flip=True)
    s3u, s3d = cross(s2u, 1, (1,)), cross(s2d, -1, (1,))
    s4 = cross(s3u, 1, (1,))

    layers = []
    for s in range(4):
        owner = (rep + s) % 4
        part = lax.dynamic_slice_in_dim(right, owner * 512, 512, 3)[:, 0]
        layers.append(part if s == 0 else lax.ppermute(part, "zhi", ring(4, s)))

    layers = jnp.stack(layers)
    other = other_core(layers)
    both = jnp.concatenate([pick(layers, other), pick(other, layers)], 2)
    near = along_x(both)
    near_o = other_core(near)
    far = along_x(pick(near[:2], near[2:]))
    far_o = other_core(far)

    m2 = join(s2d, s3u, s3d, s4)
    u2, d2 = cross(pick(u1, m2), 1, flip=True), cross(pick(d1, m2), -1, flip=True)
    u3a, d3b = cross(pick(u2[:64], u1[:64]), 1, flip=True), cross(d2[64:], -1, flip=True)
    u3b, d3a = cross(pick(u2[64:], u2[:64]), 1, flip=True), cross(pick(d2[:64], d1[64:]), -1, flip=True)

    def run(dy, dz, half):
        yy, zz = (y + dy) % 4, (z + dz) % 8
        return (((zz % 2) * 4 + yy) * 4 + zz // 2) * 2 + half

    def table(core0, core1):
        at, spare = [], [64, 64]
        for pair in zip(core0, core1, strict=True):
            both_at = []
            for c, offsets in enumerate(pair):
                both_at.append(spare[c] if offsets is None else run(*offsets))
                spare[c] += offsets is None
            at.append(pick(*both_at))
        return jnp.stack(at).astype(jnp.int32)

    def halves(*offsets):
        return [(dy, dz, half) for dy, dz in offsets for half in (0, 1)]

    none = [None, None]
    ones, twos, dys = (0, -1, 1, -2), (2, -3, 3, 4), (0, -1, 1, 2)

    def around_z(dz):
        return halves(*((dy, dz) for dy in dys))

    def around_y(dy, dzs):
        return halves(*((dy, dz) for dz in dzs))

    runs = table(
        halves((0, 0), (-1, 0), (1, 0), (2, 0))
        + none * 4
        + around_z(-1)
        + around_z(1)
        + around_z(-2)
        + around_z(2)
        + around_z(-3)
        + around_z(3)
        + around_z(4),
        halves(*((0, dz) for dz in ones + twos))
        + around_y(-1, ones)
        + around_y(1, ones)
        + around_y(-1, twos)
        + around_y(1, twos)
        + around_y(2, ones)[:4]
        + around_y(2, twos)[:4]
        + around_y(2, ones)[4:]
        + around_y(2, twos)[4:]
        + none * 4,
    )

    right_tiles = lax.dynamic_slice(right_mask, (0, col * 16 + rep * 4), (8, 4)).astype(jnp.float32)
    place = jnp.stack([x, core, rep]).astype(jnp.int32)
    right_mask = jnp.repeat(right_tiles, KT, axis=1)
    left_tiles = lax.dynamic_slice(left_mask, (0, row * 16), (8, 16)).astype(jnp.float32)
    mask = jnp.pad(jnp.repeat(left_tiles, KT, axis=1), ((0, 8), (0, 0)))

    u4, d4 = cross(u3a, 1, (0,), True), cross(d3b, -1, (0,), True)
    hi, lo = assemble_right(after(place, u1, d1), [both, near, near_o, far, far_o], right_mask)
    pieces = [left, s1u, s1d, s2u, s2d, s3u, s3d, s4, u1, d1, u2, d2, u3a, u3b, d3a, d3b, u4, d4]
    return product(runs, pieces, mask, hi, lo, accum)


def solution(mesh):
    fine = Mesh(mesh.devices.reshape(4, 2, 2, 4, 4), ("x", "core", "zlo", "y", "zhi"))
    row, col, rep = ("x", "core"), ("zlo", "y"), ("zhi",)
    return jax.shard_map(
        body,
        mesh=fine,
        in_specs=(P(col + rep, row), P(None, rep, row, col), P(), P(), P(row, col + rep)),
        out_specs=P(row, col + rep),
        check_vma=False,
    )
```

```python
import functools

import jax
import jax.numpy as jnp
from jax import lax
from jax.experimental import pallas as pl
from jax.experimental.pallas import tpu as pltpu
from jax.sharding import Mesh, PartitionSpec as P

KT = 128
RUN = 16
Z = ("zlo", "zhi")
VMEM = 56 * 2**20
TN = 512


def z_slot(z):
    return (z % 2) * 4 + z // 2


def ring(n, step, slot=lambda i: i):
    return [(slot(i), slot((i + step) % n)) for i in range(n)]


def along_x(a):
    pairs = [(i * 2 + c, (i + 1 - 2 * c) % 4 * 2 + c) for i in range(4) for c in (0, 1)]
    return lax.ppermute(a, ("x", "core"), pairs)


def other_core(a):
    return lax.ppermute(a, "core", [(0, 1), (1, 0)])


def place_of(core, z, y):
    return ((core * 2 + z % 2) * 4 + y) * 4 + z // 2


def cross(a, step, cores=(0, 1), flip=False):
    pairs = []
    for z in range(8):
        for y in range(4):
            for c in cores:
                to = (c, z, (y + step) % 4) if (c == 0) != flip else (c, (z + step) % 8, y)
                pairs.append((place_of(c, z, y), place_of(*to)))
    return lax.ppermute(a, ("core", "zlo", "y", "zhi"), pairs)


def after(a, *others):
    return lax.optimization_barrier((a,) + others)[0]


def split(a):
    h = a.astype(jnp.bfloat16)
    return h, (a - h.astype(jnp.float32)).astype(jnp.bfloat16)


def right_kernel(place, own, near, near_o, far, far_o, mask, hi, lo, rows, *refs):
    parts, sems = refs[:5], refs[5]
    x, core, rep = place[0], place[1], place[2]
    step = 2 * core - 1
    origins = ((x, 0), (x + step, 0), (x - step, 0), (x + 2, 2 * core), (x + 2, 2 - 2 * core))
    sources = (own, near, near_o, far, far_o)
    copies = [pltpu.make_async_copy(a, b, sems.at[i]) for i, (a, b) in enumerate(zip(sources, parts))]
    for copy in copies:
        copy.start()
    for copy, ref, (at_x, first) in zip(copies, parts, origins):
        copy.wait()
        for slot in range(ref.shape[0]):
            base = lax.rem(rep - first - slot + 4, 4) * 32 + lax.rem(at_x + 4, 4) * 8
            for g in range(8):
                rows[pl.ds(pl.multiple_of(g * 128 + base, 8), 8), :] = ref[slot, g]
    for g in range(8):
        at = pl.ds(g * 128, 128)
        hi[at, :], lo[at, :] = split(rows[at, :] * mask[pl.ds(g, 1), :])


def assemble_right(place, sources, mask):
    vm, hbm = pl.BlockSpec(memory_space=pltpu.VMEM), pl.BlockSpec(memory_space=pl.ANY)
    return pl.pallas_call(
        right_kernel,
        out_shape=[jax.ShapeDtypeStruct((1024, 512), jnp.bfloat16)] * 2,
        in_specs=[pl.BlockSpec(memory_space=pltpu.SMEM)] + [hbm] * 5 + [vm],
        out_specs=[vm, vm],
        scratch_shapes=[pltpu.VMEM((1024, 512), jnp.float32)]
        + [pltpu.VMEM(a.shape, jnp.float32) for a in sources]
        + [pltpu.SemaphoreType.DMA((5,))],
        compiler_params=pltpu.CompilerParams(vmem_limit_bytes=VMEM),
    )(place, *sources, mask)


def product_kernel(heights, runs, *refs):
    n = len(heights)
    tiles = 2048 // TN
    pieces, refs = refs[:n], refs[n:]
    mask, hi_in, lo_in, accum, out = refs[:5]
    held, refs = refs[5 : 5 + n], refs[5 + n :]
    hi, lo, lhi, llo, total, piece_sems, in_sems, out_sems, right_sems = refs

    def tile(i):
        return pl.ds(i * TN, TN)

    def fetches(i):
        cols = tile(i)
        copies = [
            pltpu.make_async_copy(a.at[:, cols], b.at[:, cols], piece_sems.at[i, k])
            for k, (a, b) in enumerate(zip(pieces, held))
        ]
        return copies, pltpu.make_async_copy(accum.at[cols], total.at[i], in_sems.at[i])

    right_in = [pltpu.make_async_copy(a, b, right_sems.at[i]) for i, (a, b) in enumerate(((hi_in, hi), (lo_in, lo)))]
    sends = [pltpu.make_async_copy(total.at[i], out.at[tile(i)], out_sems.at[i]) for i in range(tiles)]
    loads = [fetches(i) for i in range(tiles)]
    for copy in loads[0][0] + right_in + [loads[0][1]]:
        copy.start()
    dot = functools.partial(
        lax.dot_general, dimension_numbers=(((0,), (0,)), ((), ())), preferred_element_type=jnp.float32
    )

    def prepare(i):
        cols, slot = tile(i), i % 2
        j = 0
        for ref, height in zip(held, heights):
            for r in range(0, height, RUN):
                run = runs[j]
                there = pl.ds(pl.multiple_of(run * RUN, RUN), RUN)
                a = ref[r : r + RUN, cols] * mask[pl.ds(run // (KT // RUN), 1), cols]
                lhi[slot, there, :], llo[slot, there, :] = split(a)
                j += 1

    for copy in loads[1][0] + [loads[1][1]]:
        copy.start()
    for copy in loads[0][0]:
        copy.wait()
    prepare(0)
    for copy in right_in:
        copy.wait()
    for i in range(tiles):
        if i + 2 < tiles:
            for copy in loads[i + 2][0] + [loads[i + 2][1]]:
                copy.start()
        if i + 1 < tiles:
            for copy in loads[i + 1][0]:
                copy.wait()
        loads[i][1].wait()
        left_hi, left_lo = lhi[i % 2, :1024, :], llo[i % 2, :1024, :]
        add = dot(left_hi, lo[...]) + dot(left_lo, hi[...])
        if i + 1 < tiles:
            prepare(i + 1)
        add = add + dot(left_hi, hi[...])
        total[i] = total[i] + add
        sends[i].start()
    for copy in sends:
        copy.wait()


def product(runs, pieces, mask, hi, lo, accum):
    heights = tuple(p.shape[0] for p in pieces)
    width = pieces[0].shape[1]
    depth = sum(heights)
    tiles = width // TN
    vm, hbm = pl.BlockSpec(memory_space=pltpu.VMEM), pl.BlockSpec(memory_space=pl.ANY)
    sems = pltpu.SemaphoreType.DMA
    scratch = [pltpu.VMEM(p.shape, jnp.float32) for p in pieces]
    scratch += [pltpu.VMEM((1024, 512), jnp.bfloat16)] * 2 + [pltpu.VMEM((2, depth, TN), jnp.bfloat16)] * 2
    scratch += [pltpu.VMEM((tiles, TN, 512), jnp.float32), sems((tiles, len(pieces)))]
    scratch += [sems((tiles,)), sems((tiles,)), sems((2,))]
    return pl.pallas_call(
        functools.partial(product_kernel, heights),
        out_shape=jax.ShapeDtypeStruct(accum.shape, jnp.float32),
        in_specs=[pl.BlockSpec(memory_space=pltpu.SMEM)] + [hbm] * len(pieces) + [vm, hbm, hbm, hbm],
        out_specs=hbm,
        scratch_shapes=scratch,
        compiler_params=pltpu.CompilerParams(vmem_limit_bytes=VMEM),
        cost_estimate=pl.CostEstimate(
            flops=2 * 3 * 1024 * width * 512,
            bytes_accessed=depth * width * 4 + width * 512 * 8 + 2**21,
            transcendentals=0,
        ),
    )(runs, *pieces, mask, hi, lo, accum)


def body(left, right, left_mask, right_mask, accum):
    x, core, y = (lax.axis_index(a) for a in ("x", "core", "y"))
    zlo, rep = lax.axis_index("zlo"), lax.axis_index("zhi")
    z = rep * 2 + zlo
    row, col = x * 2 + core, zlo * 4 + y

    zero = core == 0

    def pick(a, b):
        return jnp.where(zero, a, b)

    def join(*parts):
        return jnp.concatenate(parts, 0)

    s1u, s1d = cross(left, 1), cross(left, -1)
    s2u, s2d = cross(s1u, 1), cross(s1d, -1, (1,))

    m1 = join(left, s1u, s1d)
    u1a, d1a = cross(m1, 1, flip=True), cross(m1, -1, flip=True)
    u1b, d1b = cross(s2u, 1, flip=True), cross(s2u, -1, flip=True)
    u1, d1 = join(u1a, u1b), join(d1a, d1b)
    s3u, s3d = cross(s2u, 1, (1,)), cross(s2d, -1, (1,))
    s4 = cross(s3u, 1, (1,))

    layers = []
    for s in range(4):
        owner = (rep + s) % 4
        part = lax.dynamic_slice_in_dim(right, owner * 512, 512, 3)[:, 0]
        layers.append(part if s == 0 else lax.ppermute(part, "zhi", ring(4, s)))

    layers = jnp.stack(layers)
    other = other_core(layers)
    both = jnp.concatenate([pick(layers, other), pick(other, layers)], 2)
    near = along_x(both)
    near_o = other_core(near)
    far = along_x(pick(near[:2], near[2:]))
    far_o = other_core(far)

    m2 = join(s2d, s3u, s3d, s4)
    u2, d2 = cross(pick(u1, m2), 1, flip=True), cross(pick(d1, m2), -1, flip=True)
    u3a, d3b = cross(pick(u2[:64], u1[:64]), 1, flip=True), cross(d2[64:], -1, flip=True)
    u3b, d3a = cross(pick(u2[64:], u2[:64]), 1, flip=True), cross(pick(d2[:64], d1[64:]), -1, flip=True)

    def run(dy, dz, half):
        yy, zz = (y + dy) % 4, (z + dz) % 8
        return (((zz % 2) * 4 + yy) * 4 + zz // 2) * 2 + half

    def table(core0, core1):
        at, spare = [], [64, 64]
        for pair in zip(core0, core1, strict=True):
            both_at = []
            for c, offsets in enumerate(pair):
                both_at.append(spare[c] if offsets is None else run(*offsets))
                spare[c] += offsets is None
            at.append(pick(*both_at))
        return jnp.stack(at).astype(jnp.int32)

    def halves(*offsets):
        return [(dy, dz, half) for dy, dz in offsets for half in (0, 1)]

    none = [None, None]
    ones, twos, dys = (0, -1, 1, -2), (2, -3, 3, 4), (0, -1, 1, 2)

    def around_z(dz):
        return halves(*((dy, dz) for dy in dys))

    def around_y(dy, dzs):
        return halves(*((dy, dz) for dz in dzs))

    runs = table(
        halves((0, 0), (-1, 0), (1, 0), (2, 0))
        + none * 4
        + around_z(-1)
        + around_z(1)
        + around_z(-2)
        + around_z(2)
        + around_z(-3)
        + around_z(3)
        + around_z(4),
        halves(*((0, dz) for dz in ones + twos))
        + around_y(-1, ones)
        + around_y(1, ones)
        + around_y(-1, twos)
        + around_y(1, twos)
        + around_y(2, ones)[:4]
        + around_y(2, twos)[:4]
        + around_y(2, ones)[4:]
        + around_y(2, twos)[4:]
        + none * 4,
    )

    right_tiles = lax.dynamic_slice(right_mask, (0, col * 16 + rep * 4), (8, 4)).astype(jnp.float32)
    place = jnp.stack([x, core, rep]).astype(jnp.int32)
    right_mask = jnp.repeat(right_tiles, KT, axis=1)
    left_tiles = lax.dynamic_slice(left_mask, (0, row * 16), (8, 16)).astype(jnp.float32)
    mask = jnp.pad(jnp.repeat(left_tiles, KT, axis=1), ((0, 8), (0, 0)))

    u4, d4 = cross(u3a, 1, (0,), True), cross(d3b, -1, (0,), True)
    hi, lo = assemble_right(after(place, u1a, d1a), [both, near, near_o, far, far_o], right_mask)
    pieces = [left, s1u, s1d, s2u, s2d, s3u, s3d, s4, u1a, u1b, d1a, d1b, u2, d2, u3a, u3b, d3a, d3b, u4, d4]
    return product(runs, pieces, mask, hi, lo, accum)


def solution(mesh):
    fine = Mesh(mesh.devices.reshape(4, 2, 2, 4, 4), ("x", "core", "zlo", "y", "zhi"))
    row, col, rep = ("x", "core"), ("zlo", "y"), ("zhi",)
    return jax.shard_map(
        body,
        mesh=fine,
        in_specs=(P(col + rep, row), P(None, rep, row, col), P(), P(), P(row, col + rep)),
        out_specs=P(row, col + rep),
        check_vma=False,
    )
```
